32 devices in a mesh: gz: 2 (over x), gy: 16 (over z, y, core).
Axes of the slice: x: 2, y: 2, z: 4, core: 2. Of those that a mesh axis runs over, the one named last changes fastest.
Arguments:
- observed: float32 [64, 512, 768], P('gz', 'gy'), may hold values from 0.2 to 5
- estimate: float32 [64, 512, 768], P('gz', 'gy'), may hold values from 0.5 to 2
- taps_z: float32 [9], replicated, may hold values from 0.05 to 1
- taps_y: float32 [9], replicated, may hold values from 0.05 to 1
- taps_x: float32 [9], replicated, may hold values from 0.05 to 1
Outputs:
- updated: float32 [64, 512, 768], P('gz', 'gy')
- projection: float32 [512, 768], P('gy')
The draws below stay inside these ranges and needn't reach their ends.
All inputs are finite; a program needn't handle non-finite values.
Results may differ from the reference program's by a relative error of at most 0.00002.
Values sent between devices are 32-bit elements; how exact they have to be, the bound alone decides.
A program may use at most 64 MiB of HBM per device.

```python
import math
import jax
import jax.numpy as jnp
from jax import lax

XCELLS = 768
TAPS = 9
YCELLS = 512
ZCELLS = 64


def block_levels(key, extent, shards, least, top_value):
    gain = 1.0
    for position, parts in shards:
        heights = jax.random.uniform(jax.random.fold_in(jax.random.fold_in(key, 6), position), (parts,), jnp.float32, least / len(shards), top_value / len(shards))
        gain = gain * jnp.repeat(jnp.exp(heights), extent[position] // parts).reshape((-1,) + (1,) * (len(extent) - 1 - position))
    return gain


def setup_inputs(seed: int = 0) -> dict:
    streams_of = jax.random.split(jax.random.key(seed), 6)
    return {
        "observed": jnp.clip(jnp.exp(math.log(5.0) - 3.218876 * jax.random.uniform(streams_of[0], (ZCELLS, YCELLS, XCELLS), jnp.float32) ** block_levels(streams_of[0], (ZCELLS, YCELLS, XCELLS), ((0, 2), (1, 16)), -0.2, 0.2)), 0.2, 5.0),
        "estimate": jnp.clip(jnp.exp(math.log(2.0) - 1.3862944 * jax.random.uniform(streams_of[1], (ZCELLS, YCELLS, XCELLS), jnp.float32) ** block_levels(streams_of[1], (ZCELLS, YCELLS, XCELLS), ((0, 2), (1, 16)), -0.2, 0.2)), 0.5, 2.0),
        "taps_z": jnp.clip(jnp.exp(jax.random.uniform(streams_of[2], (TAPS,), jnp.float32, math.log(0.05), math.log(1.0))), 0.05, 1.0),
        "taps_y": jnp.clip(jnp.exp(jax.random.uniform(streams_of[3], (TAPS,), jnp.float32, math.log(0.05), math.log(1.0))), 0.05, 1.0),
        "taps_x": jnp.clip(jnp.exp(jax.random.uniform(streams_of[4], (TAPS,), jnp.float32, math.log(0.05), math.log(1.0))), 0.05, 1.0),
    }


def blur_axis(volume, taps, axis):
    radius = (taps.shape[0] - 1) // 2
    count = volume.shape[axis]
    widths = [(0, 0), (0, 0), (0, 0)]
    widths[axis] = (radius, radius)
    padded = jnp.pad(volume, widths)
    total = taps[0] * lax.slice_in_dim(padded, 0, count, axis=axis)
    for index in range(1, taps.shape[0]):
        total = total + taps[index] * lax.slice_in_dim(padded, index, index + count, axis=axis)
    return total


def blur_volume(volume, taps_z, taps_y, taps_x):
    volume = blur_axis(volume, taps_z, 0)
    volume = blur_axis(volume, taps_y, 1)
    return blur_axis(volume, taps_x, 2)


def reference(observed, estimate, taps_z, taps_y, taps_x):
    blurred = blur_volume(estimate, taps_z, taps_y, taps_x)
    ratio = observed / blurred
    correction = blur_volume(ratio, taps_z[::-1], taps_y[::-1], taps_x[::-1])
    updated = estimate * correction
    projection = jnp.max(updated, axis=0)
    return updated, projection
```

```python
import functools

import jax
import jax.numpy as jnp
from jax import lax
from jax.experimental import pallas as pl
from jax.experimental.pallas import tpu as pltpu
from jax.sharding import PartitionSpec as P

F32 = jnp.float32
BF16 = jnp.bfloat16
MESH = pl.DeviceIdType.MESH
DIRS = tuple((dz, dy) for dz in (-1, 0, 1) for dy in (-1, 0, 1) if (dz, dy) != (0, 0))


def split(v):
    hi = v.astype(BF16)
    lo = (v - hi.astype(F32)).astype(BF16)
    return hi, lo


def kernel(nz, ny, obs_hbm, est_hbm, wz_ref, wy_ref, wx_ref, out_ref, proj_ref,
           est_pad, rat_pad, mid, obs, band_x, band_y, mx_all,
           e_send, e_recv, r_send, r_recv, p_send, p_recv, l_sem):
    taps = wz_ref.shape[0]
    rad = (taps - 1) // 2
    Z, Y, X = obs.shape
    OFF = 8
    gz, gy = lax.axis_index("gz"), lax.axis_index("gy")

    def valid(dz, dy):
        z, y = gz + dz, gy + dy
        return (z >= 0) & (z < nz) & (y >= 0) & (y < ny)

    load_est = pltpu.make_async_copy(
        est_hbm, est_pad.at[pl.ds(rad, Z), pl.ds(OFF, Y), :], l_sem.at[0])
    load_obs = pltpu.make_async_copy(obs_hbm, obs, l_sem.at[1])
    load_est.start()
    load_obs.start()

    barrier = pltpu.get_barrier_semaphore()
    for buf in (est_pad, rat_pad):
        buf[:, 0:OFF, :] = jnp.zeros((Z + 2 * rad, OFF, X), F32)
        buf[:, OFF + Y:, :] = jnp.zeros((Z + 2 * rad, OFF, X), F32)

        @pl.when(gz == 0)
        def _():
            buf[0:rad, OFF:OFF + Y, :] = jnp.zeros((rad, Y, X), F32)

        @pl.when(gz == nz - 1)
        def _():
            buf[rad + Z:, OFF:OFF + Y, :] = jnp.zeros((rad, Y, X), F32)

    count = jnp.int32(nz - 1)
    for dz, dy in DIRS:
        ok = valid(dz, dy)
        count = count + ok.astype(jnp.int32)

        @pl.when(ok)
        def _():
            pl.semaphore_signal(barrier, inc=1, device_id=(gz + dz, gy + dy), device_id_type=MESH)
    for d in range(1, nz):
        pl.semaphore_signal(barrier, inc=1, device_id=(lax.rem(gz + d, nz), gy), device_id_type=MESH)
    pl.semaphore_wait(barrier, count)

    def span(d, n, width):
        if d == 0:
            return pl.ds(0, n), pl.ds(0, n)
        if d > 0:
            return pl.ds(n - width, width), pl.ds(-width, width)
        return pl.ds(0, width), pl.ds(n, width)

    def shifted(s, off):
        return pl.ds(s.start + off, s.size)

    def halo(src, zo, yo, pad, send, recv):
        copies = []
        for i, (dz, dy) in enumerate(DIRS):
            sz, tz = span(dz, Z, rad)
            sy, ty = span(dy, Y, rad)
            copies.append((dz, dy, pltpu.make_async_remote_copy(
                src_ref=src.at[shifted(sz, zo), shifted(sy, yo), :],
                dst_ref=pad.at[shifted(tz, rad), shifted(ty, OFF), :],
                send_sem=send.at[i], recv_sem=recv.at[i],
                device_id=(gz + dz, gy + dy), device_id_type=MESH)))
        return copies

    def start(copies):
        for dz, dy, c in copies:
            @pl.when(valid(dz, dy))
            def _():
                c.start()

    def wait_recv(copies):
        for dz, dy, c in copies:
            @pl.when(valid(-dz, -dy))
            def _():
                c.wait_recv()

    def wait_send(copies):
        for dz, dy, c in copies:
            @pl.when(valid(dz, dy))
            def _():
                c.wait_send()

    e_copies = halo(est_hbm, 0, 0, est_pad, e_send, e_recv)
    start(e_copies)

    def band(shape, off, w_ref, back):
        diff = lax.broadcasted_iota(jnp.int32, shape, 0) - lax.broadcasted_iota(jnp.int32, shape, 1)
        total = jnp.zeros(shape, F32)
        for k in range(taps):
            w = w_ref[taps - 1 - k] if back else w_ref[k]
            total = jnp.where(diff == off + k, w, total)
        return total

    for b in range(2):
        hi, lo = split(band((512, 256), 128 - rad, wx_ref, b))
        band_x[b, 0] = hi
        band_x[b, 1] = lo
        diff = (lax.broadcasted_iota(jnp.int32, (Y, Y + 2 * OFF), 1)
                - lax.broadcasted_iota(jnp.int32, (Y, Y + 2 * OFF), 0))
        total = jnp.zeros(diff.shape, F32)
        for k in range(taps):
            w = wy_ref[taps - 1 - k] if b else wy_ref[k]
            total = jnp.where(diff == OFF - rad + k, w, total)
        hi, lo = split(total)
        band_y[b] = jnp.concatenate([hi, hi, lo], axis=1)

    def z_pass(pad, back):
        ws = [wz_ref[taps - 1 - k] if back else wz_ref[k] for k in range(taps)]
        nc = X // 128

        def body(i, _):
            r = pl.ds(pl.multiple_of((i // nc) * 8, 8), 8)
            c = pl.ds(pl.multiple_of(lax.rem(i, nc) * 128, 128), 128)
            vals = [pad[p, r, c] for p in range(Z + taps - 1)]
            for z in range(Z):
                t = ws[0] * vals[z]
                for k in range(1, taps):
                    t = t + ws[k] * vals[z + k]
                mid[z, r, c] = t
            return 0

        lax.fori_loop(0, (Y // 8 + 2) * nc, body, 0)

    G = 4
    NT = 256

    def yx_pass(back, use):
        def body(g, carry):
            rows = []
            for j in range(G):
                hi, lo = split(mid[g * G + j])
                rhs = jnp.concatenate([hi, lo, hi], axis=0)
                rows.append(jnp.dot(band_y[back], rhs, preferred_element_type=F32))
            hi, lo = split(jnp.concatenate(rows, axis=0))
            for n in range(X // NT):
                k0, k1 = max(n * NT - 128, 0), min(n * NT + NT + 128, X)
                b0 = k0 - (n * NT - 128)
                th = band_x[back, 0, b0:b0 + k1 - k0, :]
                tl = band_x[back, 1, b0:b0 + k1 - k0, :]
                h, l = hi[:, k0:k1], lo[:, k0:k1]
                t = (jnp.dot(h, th, preferred_element_type=F32)
                     + jnp.dot(l, th, preferred_element_type=F32)
                     + jnp.dot(h, tl, preferred_element_type=F32))
                use(g, pl.ds(n * NT, NT), t.reshape(G, Y, NT))
            return carry

        lax.fori_loop(0, Z // G, body, 0)

    load_est.wait()
    wait_recv(e_copies)
    z_pass(est_pad, 0)
    load_obs.wait()

    def use_ratio(g, c, t):
        rat_pad[pl.ds(rad + g * G, G), OFF:OFF + Y, c] = obs[pl.ds(g * G, G), :, c] / t

    yx_pass(0, use_ratio)

    r_copies = halo(rat_pad, rad, OFF, rat_pad, r_send, r_recv)
    start(r_copies)
    wait_recv(r_copies)
    z_pass(rat_pad, 1)

    mx_all[0] = jnp.full((Y, X), -jnp.inf, F32)

    def use_corr(g, c, t):
        u = est_pad[pl.ds(rad + g * G, G), OFF:OFF + Y, c] * t
        out_ref[pl.ds(g * G, G), :, c] = u
        mx_all[0, :, c] = jnp.maximum(mx_all[0, :, c], jnp.max(u, axis=0))

    yx_pass(1, use_corr)

    p_copies = []
    for d in range(1, nz):
        c = pltpu.make_async_remote_copy(
            src_ref=mx_all.at[0], dst_ref=mx_all.at[d],
            send_sem=p_send.at[d - 1], recv_sem=p_recv.at[d - 1],
            device_id=(lax.rem(gz + d, nz), gy), device_id_type=MESH)
        c.start()
        p_copies.append(c)
    best = mx_all[0]
    for d, c in enumerate(p_copies):
        c.wait_recv()
        best = jnp.maximum(best, mx_all[d + 1])
    proj_ref[...] = best
    wait_send(e_copies)
    wait_send(r_copies)
    for c in p_copies:
        c.wait_send()


def per_device(nz, ny, observed, estimate, taps_z, taps_y, taps_x):
    Z, Y, X = observed.shape
    taps = taps_z.shape[0]
    rad = (taps - 1) // 2
    pad = (Z + 2 * rad, Y + 16, X)
    nd = len(DIRS)
    smem = pl.BlockSpec(memory_space=pltpu.SMEM)
    hbm = pl.BlockSpec(memory_space=pl.ANY)
    vmem = pl.BlockSpec(memory_space=pltpu.VMEM)
    dma = pltpu.SemaphoreType.DMA
    return pl.pallas_call(
        functools.partial(kernel, nz, ny),
        out_shape=(jax.ShapeDtypeStruct((Z, Y, X), F32), jax.ShapeDtypeStruct((Y, X), F32)),
        in_specs=[hbm, hbm, smem, smem, smem],
        out_specs=(vmem, vmem),
        scratch_shapes=[
            pltpu.VMEM(pad, F32),
            pltpu.VMEM(pad, F32),
            pltpu.VMEM((Z, Y + 16, X), F32),
            pltpu.VMEM((Z, Y, X), F32),
            pltpu.VMEM((2, 2, 512, 256), BF16),
            pltpu.VMEM((2, Y, 3 * (Y + 16)), BF16),
            pltpu.VMEM((nz, Y, X), F32),
            dma((nd,)), dma((nd,)), dma((nd,)), dma((nd,)),
            dma((nz - 1,)), dma((nz - 1,)), dma((2,)),
        ],
        compiler_params=pltpu.CompilerParams(
            collective_id=0, has_side_effects=True, vmem_limit_bytes=50 * 1024 * 1024),
        name="deconvolve",
    )(observed, estimate, taps_z, taps_y, taps_x)


def solution(mesh):
    return jax.shard_map(
        functools.partial(per_device, mesh.shape["gz"], mesh.shape["gy"]),
        mesh=mesh,
        in_specs=(P("gz", "gy", None), P("gz", "gy", None), P(), P(), P()),
        out_specs=(P("gz", "gy", None), P("gy", None)),
        check_vma=False,
    )
```

```python
import functools

import jax
import jax.numpy as jnp
from jax import lax
from jax.experimental import pallas as pl
from jax.experimental.pallas import tpu as pltpu
from jax.sharding import PartitionSpec as P

F32 = jnp.float32
BF16 = jnp.bfloat16
MESH = pl.DeviceIdType.MESH
DIRS = tuple((dz, dy) for dz in (-1, 0, 1) for dy in (-1, 0, 1) if (dz, dy) != (0, 0))


def split(v):
    hi = v.astype(BF16)
    lo = (v - hi.astype(F32)).astype(BF16)
    return hi, lo


def kernel(nz, ny, cw, obs_hbm, est_hbm, wz_hbm, wy_hbm, wx_hbm, out, proj_ref,
           est_pad, rat_pad, mid, yh, yl, obs, band_x, band_y, mx_all, w_ref,
           e_send, e_recv, r_send, r_recv, p_send, p_recv, l_sem, w_sem):
    taps = w_ref.shape[1]
    rad = (taps - 1) // 2
    Z, Y, X = obs.shape
    OFF = 8
    NC = X // cw
    gz, gy = lax.axis_index("gz"), lax.axis_index("gy")

    def valid(dz, dy):
        z, y = gz + dz, gy + dy
        return (z >= 0) & (z < nz) & (y >= 0) & (y < ny)

    def cols(c):
        return pl.ds(c * cw, cw)

    w_loads = [pltpu.make_async_copy(w, w_ref.at[i], w_sem.at[i])
               for i, w in enumerate((wz_hbm, wy_hbm, wx_hbm))]
    for c in w_loads:
        c.start()
    est_loads, obs_loads = [], []
    for c in range(NC):
        est_loads.append(pltpu.make_async_copy(
            est_hbm.at[:, :, cols(c)], est_pad.at[pl.ds(rad, Z), pl.ds(OFF, Y), cols(c)],
            l_sem.at[c]))
        obs_loads.append(pltpu.make_async_copy(
            obs_hbm.at[:, :, cols(c)], obs.at[:, :, cols(c)], l_sem.at[NC + c]))

    barrier = pltpu.get_barrier_semaphore()
    for buf in (est_pad, rat_pad):
        buf[:, 0:OFF, :] = jnp.zeros((Z + 2 * rad, OFF, X), F32)
        buf[:, OFF + Y:, :] = jnp.zeros((Z + 2 * rad, OFF, X), F32)

        @pl.when(gz == 0)
        def _():
            buf[0:rad, OFF:OFF + Y, :] = jnp.zeros((rad, Y, X), F32)

        @pl.when(gz == nz - 1)
        def _():
            buf[rad + Z:, OFF:OFF + Y, :] = jnp.zeros((rad, Y, X), F32)

    count = jnp.int32(nz - 1)
    for dz, dy in DIRS:
        ok = valid(dz, dy)
        count = count + ok.astype(jnp.int32)

        @pl.when(ok)
        def _():
            pl.semaphore_signal(barrier, inc=1, device_id=(gz + dz, gy + dy), device_id_type=MESH)
    for d in range(1, nz):
        pl.semaphore_signal(barrier, inc=1, device_id=(lax.rem(gz + d, nz), gy), device_id_type=MESH)
    pl.semaphore_wait(barrier, count)

    def span(d, n, width):
        if d == 0:
            return (0, n), (0, n)
        if d > 0:
            return (n - width, width), (-width, width)
        return (0, width), (n, width)

    def shifted(s, off):
        return pl.ds(s[0] + off, s[1])

    def halo(c, src, zo, yo, pad, send, recv):
        copies = []
        for i, (dz, dy) in enumerate(DIRS):
            sz, tz = span(dz, Z, rad)
            sy, ty = span(dy, Y, rad)
            copies.append((dz, dy, pltpu.make_async_remote_copy(
                src_ref=src.at[shifted(sz, zo), shifted(sy, yo), cols(c)],
                dst_ref=pad.at[shifted(tz, rad), shifted(ty, OFF), cols(c)],
                send_sem=send.at[c * len(DIRS) + i], recv_sem=recv.at[c * len(DIRS) + i],
                device_id=(gz + dz, gy + dy), device_id_type=MESH)))
        return copies

    def start(copies):
        for dz, dy, c in copies:
            @pl.when(valid(dz, dy))
            def _():
                c.start()

    def wait_recv(copies):
        for dz, dy, c in copies:
            @pl.when(valid(-dz, -dy))
            def _():
                c.wait_recv()

    def wait_send(copies):
        for dz, dy, c in copies:
            @pl.when(valid(dz, dy))
            def _():
                c.wait_send()

    e_copies = [halo(c, est_hbm, 0, 0, est_pad, e_send, e_recv) for c in range(NC)]
    r_copies = [halo(c, rat_pad, rad, OFF, rat_pad, r_send, r_recv) for c in range(NC)]
    start(e_copies[0])
    for c in range(NC):
        est_loads[c].start()
    for c in range(NC):
        obs_loads[c].start()

    for c in w_loads:
        c.wait()

    def weight(dim, k, back):
        return w_ref[dim, taps - 1 - k if back else k]

    for b in range(2):
        diff = (lax.broadcasted_iota(jnp.int32, band_x.shape[2:], 0)
                - lax.broadcasted_iota(jnp.int32, band_x.shape[2:], 1))
        total = jnp.zeros(diff.shape, F32)
        for k in range(taps):
            total = jnp.where(diff == 128 - rad + k, weight(2, k, b), total)
        hi, lo = split(total)
        band_x[b, 0] = hi
        band_x[b, 1] = lo
        diff = (lax.broadcasted_iota(jnp.int32, (Y, Y + 2 * OFF), 1)
                - lax.broadcasted_iota(jnp.int32, (Y, Y + 2 * OFF), 0))
        total = jnp.zeros(diff.shape, F32)
        for k in range(taps):
            total = jnp.where(diff == OFF - rad + k, weight(1, k, b), total)
        hi, lo = split(total)
        band_y[b] = jnp.concatenate([hi, hi, lo], axis=1)

    def z_pass(pad, back, c):
        ws = [weight(0, k, back) for k in range(taps)]
        nl = cw // 128

        def body(i, _):
            r = pl.ds(pl.multiple_of((i // nl) * 8, 8), 8)
            lane = lax.rem(i, nl) * 128
            src = pl.ds(pl.multiple_of(c * cw + lane, 128), 128)
            dst = pl.ds(pl.multiple_of(lane, 128), 128)
            vals = [pad[p, r, src] for p in range(Z + taps - 1)]
            for z in range(Z):
                t = ws[0] * vals[z]
                for k in range(1, taps):
                    t = t + ws[k] * vals[z + k]
                mid[z, r, dst] = t
            return 0

        lax.fori_loop(0, (Y // 8 + 2) * nl, body, 0)

    G = min(16, Z)

    def y_pass(back, c):
        def body(g, carry):
            rows = []
            for j in range(G):
                hi, lo = split(mid[g * G + j])
                rhs = jnp.concatenate([hi, lo, hi], axis=0)
                rows.append(jnp.dot(band_y[back], rhs, preferred_element_type=F32))
            hi, lo = split(jnp.concatenate(rows, axis=0))
            r = pl.ds(pl.multiple_of(g * G * Y, G * Y), G * Y)
            yh[r, cols(c)] = hi
            yl[r, cols(c)] = lo
            return carry

        lax.fori_loop(0, Z // G, body, 0)

    def x_pass(back, c, use):
        k0, k1 = max(c * cw - 128, 0), min(c * cw + cw + 128, X)
        b0 = k0 - (c * cw - 128)

        def body(g, carry):
            r = pl.ds(pl.multiple_of(g * G * Y, G * Y), G * Y)
            th = band_x[back, 0, b0:b0 + k1 - k0, :]
            tl = band_x[back, 1, b0:b0 + k1 - k0, :]
            h, l = yh[r, k0:k1], yl[r, k0:k1]
            t = (jnp.dot(h, th, preferred_element_type=F32)
                 + jnp.dot(l, th, preferred_element_type=F32)
                 + jnp.dot(h, tl, preferred_element_type=F32))
            use(g, t.reshape(G, Y, cw))
            return carry

        lax.fori_loop(0, Z // G, body, 0)

    def ratio_chunk(c):
        def use(g, t):
            rat_pad[pl.ds(rad + g * G, G), OFF:OFF + Y, cols(c)] = obs[pl.ds(g * G, G), :, cols(c)] / t

        obs_loads[c].wait()
        x_pass(0, c, use)
        start(r_copies[c])

    for c in range(NC):
        est_loads[c].wait()
        wait_send(e_copies[c])
        if c + 1 < NC:
            start(e_copies[c + 1])
        wait_recv(e_copies[c])
        z_pass(est_pad, 0, c)
        y_pass(0, c)
        if c > 0:
            ratio_chunk(c - 1)
    ratio_chunk(NC - 1)

    p_copies = []

    def update_chunk(c):
        mx_all[0, :, cols(c)] = jnp.full((Y, cw), -jnp.inf, F32)

        def use(g, t):
            u = est_pad[pl.ds(rad + g * G, G), OFF:OFF + Y, cols(c)] * t
            out[pl.ds(g * G, G), :, cols(c)] = u
            mx_all[0, :, cols(c)] = jnp.maximum(mx_all[0, :, cols(c)], jnp.max(u, axis=0))

        x_pass(1, c, use)
        for d in range(1, nz):
            i = c * (nz - 1) + d - 1
            copy = pltpu.make_async_remote_copy(
                src_ref=mx_all.at[0, :, cols(c)], dst_ref=mx_all.at[d, :, cols(c)],
                send_sem=p_send.at[i], recv_sem=p_recv.at[i],
                device_id=(lax.rem(gz + d, nz), gy), device_id_type=MESH)
            copy.start()
            p_copies.append(copy)

    for c in range(NC):
        wait_recv(r_copies[c])
        z_pass(rat_pad, 1, c)
        y_pass(1, c)
        if c > 0:
            update_chunk(c - 1)
    update_chunk(NC - 1)

    for copies in r_copies:
        wait_send(copies)
    for copy in p_copies:
        copy.wait_recv()
    best = mx_all[0]
    for d in range(1, nz):
        best = jnp.maximum(best, mx_all[d])
    proj_ref[...] = best
    for copy in p_copies:
        copy.wait_send()


def per_device(nz, ny, observed, estimate, taps_z, taps_y, taps_x):
    Z, Y, X = observed.shape
    taps = taps_z.shape[0]
    rad = (taps - 1) // 2
    pad = (Z + 2 * rad, Y + 16, X)
    cw = 256
    nc = X // cw
    nd = nc * len(DIRS)
    hbm = pl.BlockSpec(memory_space=pltpu.HBM)
    vmem = pl.BlockSpec(memory_space=pltpu.VMEM)
    dma = pltpu.SemaphoreType.DMA
    return pl.pallas_call(
        functools.partial(kernel, nz, ny, cw),
        out_shape=(jax.ShapeDtypeStruct((Z, Y, X), F32), jax.ShapeDtypeStruct((Y, X), F32)),
        in_specs=[hbm] * 5,
        out_specs=(vmem, vmem),
        scratch_shapes=[
            pltpu.VMEM(pad, F32),
            pltpu.VMEM(pad, F32),
            pltpu.VMEM((Z, Y + 16, cw), F32),
            pltpu.VMEM((Z * Y, X), BF16),
            pltpu.VMEM((Z * Y, X), BF16),
            pltpu.VMEM((Z, Y, X), F32),
            pltpu.VMEM((2, 2, cw + 256, cw), BF16),
            pltpu.VMEM((2, Y, 3 * (Y + 16)), BF16),
            pltpu.VMEM((nz, Y, X), F32),
            pltpu.SMEM((3, taps), F32),
            dma((nd,)), dma((nd,)), dma((nd,)), dma((nd,)),
            dma((nc * (nz - 1),)), dma((nc * (nz - 1),)), dma((2 * nc,)), dma((3,)),
        ],
        compiler_params=pltpu.CompilerParams(
            collective_id=0, has_side_effects=True, vmem_limit_bytes=50 * 1024 * 1024),
        name="deconvolve",
    )(observed, estimate, taps_z, taps_y, taps_x)


def solution(mesh):
    return jax.shard_map(
        functools.partial(per_device, mesh.shape["gz"], mesh.shape["gy"]),
        mesh=mesh,
        in_specs=(P("gz", "gy", None), P("gz", "gy", None), P(), P(), P()),
        out_specs=(P("gz", "gy", None), P("gy", None)),
        check_vma=False,
    )
```
